32 devices in a mesh: groups: 2 (over y), tensor: 8 (over z, x), context: 2 (over core).
Axes of the slice: x: 2, y: 2, z: 4, core: 2. Of those that a mesh axis runs over, the one named last changes fastest.
Arguments:
- activations: bfloat16 [16384, 28672], P(('groups', 'context'), 'tensor'), parts along dimension 0, may hold values from -6 to 6
- out_grads: bfloat16 [16384, 8192], P(('groups', 'context'), 'tensor'), parts along dimension 0, may hold values from -6 to 6
- basis_in: bfloat16 [28672, 64], P('tensor'), may hold values from -0.03125 to 0.03125
- basis_out: bfloat16 [8192, 64], P('tensor'), may hold values from -0.0625 to 0.0625
- val_sketches: bfloat16 [512, 4096], P('tensor'), may hold values from -0.01171875 to 0.01171875
- val_owner: int32 [512], P('tensor'), may hold values from 0 to 511, each once
- example_ids: int32 [256], P(('groups', 'context')), parts along dimension 0, may hold values from 0 to 63, never falling along the last dimension, each value on 1 to 4 neighbouring positions
Outputs:
- sketches: bfloat16 [128, 4096], P('groups'), parts along dimension 0
- scores: float32 [128, 512], P('groups', 'tensor'), parts along dimension 0
The draws below stay inside these ranges and needn't reach their ends.
There are 2 independent parts, one for each index of `groups`. The reference program is written for one: setup_inputs(seed, part) draws one part's arguments, and reference() takes and returns one part's arrays. A program takes and returns all parts, laid end to end along the dimension named above; an argument that names none is the same for every part. Nothing has to cross between parts.
Inputs may be any that keep to these rules, and one draw needn't show every extreme that they name: `val_owner`: a permutation of the stored rows. `example_ids`: never falling along the sequence; each example covers 1 to 4 blocks, one exactly 4; every example is present.
All inputs are finite; a program needn't handle non-finite values.
Results may differ from the reference program's by a relative error of at most 0.0059.
Values may be sent and summed in bfloat16 or wider, within the bound.
A program may use at most 128 MiB of HBM per device.

```python
import math
import jax
import jax.numpy as jnp
import numpy as np
from jax import lax

IN = 28672
OUT = 8192
RANK = 64
SKETCH = 4096
BLOCK = 64
MOST_BLOCKS = 4
VAL = 512
TOKENS = 8192
NBLOCKS = 128
EXAMPLES = 64


def block_scale(stream_key, dims, pieces, least, top_value):
    loudness, own = 1.0, jax.random.fold_in(stream_key, 6)
    for position, shards_of in pieces:
        heights = jnp.exp(jax.random.uniform(jax.random.fold_in(own, position), (shards_of,), jnp.float32, least / len(pieces), top_value / len(pieces)))
        loudness = loudness * jnp.repeat(heights, dims[position] // shards_of).reshape([-1 if axis == position else 1 for axis in range(len(dims))])
    return loudness


def profile(number_of, total, reach, skew):
    loads = [(1 << 20) // math.isqrt(rank ** skew) + 1 for rank in range(2, number_of + 1)]
    rest, holding = total - reach - (number_of - 1), [1] * (number_of - 1)
    while rest > 0:
        free = [i for i in range(number_of - 1) if holding[i] < reach]
        pool, remaining = sum([loads[i] for i in free]), rest
        for i in free:
            addition = min(reach - holding[i], max(1, remaining * loads[i] // pool), rest)
            holding[i] = holding[i] + addition
            rest = rest - addition
    return np.array([reach] + holding)


def uneven(stream_key, count, total, reach, slope):
    if count == 2:
        one = jax.random.randint(stream_key, (), max(1, total - reach), min(reach, total - 1) + 1)
        return jnp.stack([one, total - one])
    tallies = jnp.asarray(profile(count, total, reach, slope), jnp.int32)
    pairs = (count - 1) // 2
    giver, sink = tallies[1:1 + 2 * pairs:2], tallies[2:2 + 2 * pairs:2]
    margin = jnp.minimum(giver - 1, reach - sink)
    passed = jax.random.randint(jax.random.fold_in(stream_key, 1), (pairs,), 0, 1 << 20) % (margin + 1)
    tallies = tallies.at[1:1 + 2 * pairs:2].set(giver - passed).at[2:2 + 2 * pairs:2].set(sink + passed)
    return tallies[jax.random.permutation(jax.random.fold_in(stream_key, 2), count)]


def gaussian(stream_key, extent, scale, most, shards=(), held_as=jnp.bfloat16):
    values = scale * jax.random.normal(stream_key, extent, jnp.float32)
    if shards:
        values = values * block_scale(stream_key, extent, shards, -0.22, 0.18)
    return jnp.clip(values, -most, most).astype(held_as)


def setup_inputs(seed: int = 0, part: int = 0) -> dict:
    keys = jax.random.split(jax.random.key(seed), 8)
    own_keys = jax.random.split(jax.random.fold_in(keys[7], part), 8)
    return {
        "activations": gaussian(own_keys[0], (TOKENS, IN), 1.0, 6.0, ((0, 2), (1, 8))),
        "out_grads": gaussian(own_keys[1], (TOKENS, OUT), 1.0, 6.0, ((0, 2), (1, 8))),
        "basis_in": gaussian(keys[2], (IN, RANK), IN ** -0.5, 0.03125, ((0, 8),)),
        "basis_out": gaussian(keys[3], (OUT, RANK), OUT ** -0.5, 0.0625, ((0, 8),)),
        "val_sketches": gaussian(keys[4], (VAL, SKETCH), (SKETCH * 64) ** -0.5, 0.01171875, ((0, 8),)),
        "val_owner": jax.random.permutation(keys[5], VAL).astype(jnp.int32),
        "example_ids": jnp.searchsorted(jnp.cumsum(uneven(own_keys[6], EXAMPLES, NBLOCKS, MOST_BLOCKS, 2)), jnp.arange(NBLOCKS), side="right").astype(jnp.int32),
    }


def reference(activations, out_grads, basis_in, basis_out, val_sketches, val_owner, example_ids):
    proj_in = jnp.dot(activations, basis_in, preferred_element_type=jnp.float32).astype(jnp.bfloat16)
    proj_out = jnp.dot(out_grads, basis_out, preferred_element_type=jnp.float32).astype(jnp.bfloat16)
    left = proj_in.astype(jnp.float32).reshape(NBLOCKS, BLOCK, RANK)
    right = proj_out.astype(jnp.float32).reshape(NBLOCKS, BLOCK, RANK)
    outer = jnp.einsum('kta,ktb->kab', left, right).reshape(NBLOCKS, SKETCH)
    member = (example_ids[:, None] == jnp.arange(EXAMPLES, dtype=jnp.int32)[None, :]).astype(jnp.float32)
    summed = lax.dot_general(member, outer, (((0,), (0,)), ((), ())), precision=lax.Precision.HIGHEST)
    sketches = summed.astype(jnp.bfloat16)
    chosen = val_sketches[val_owner]
    scores = lax.dot_general(sketches, chosen, (((1,), (1,)), ((), ())), preferred_element_type=jnp.float32)
    return sketches, scores
```

```python
import functools

import jax
import jax.numpy as jnp
from jax import lax
from jax.experimental import pallas as pl
from jax.experimental.pallas import tpu as pltpu
from jax.sharding import PartitionSpec as P

MESH = pl.DeviceIdType.MESH
F32, BF16 = jnp.float32, jnp.bfloat16
BUFFERS = 3


def one_hot(rows, columns, hit):
    row = lax.broadcasted_iota(jnp.int32, (rows, columns), 0)
    column = lax.broadcasted_iota(jnp.int32, (rows, columns), 1)
    return jnp.where(hit(row, column), 1.0, 0.0).astype(BF16)


def kernel(
    size, slots, act, grads, basis_in, basis_out, val, owner, ids, sketches, scores,
    abuf, gbuf, wide_in, wide_out, sent, xbuf, zbuf, acc, terms, firsts, held, pieces,
    act_sem, grad_sem, x_send, x_recv, z_send, z_recv, first_send, first_recv,
    gx_send, gz_send, gc_send, g_recv, s_send, s_recv,
):
    c = lax.axis_index("context")
    t = lax.axis_index("tensor")
    half = size // 2
    rows = acc.shape[0]
    rank = basis_in.shape[1]
    examples = sketches.shape[0]
    parity, mine = t % 2, t // 2
    pair = t + 1 - 2 * parity
    other = 1 - c
    nblock = ids.shape[0]
    block = rows * size // nblock

    def peer(j):
        return (mine + 1 + j) % half

    def target(i):
        side = jnp.where(i < half, 1 - parity, parity)
        return 2 * peer(i % half) + side

    def load(i):
        slot = i % BUFFERS
        start = pl.multiple_of(target(i) * rows, rows)
        return (
            pltpu.make_async_copy(act.at[pl.ds(start, rows), :], abuf.at[slot], act_sem.at[slot]),
            pltpu.make_async_copy(grads.at[pl.ds(start, rows), :], gbuf.at[slot], grad_sem.at[slot]),
        )

    def begin(i):
        for copy in load(i):
            copy.start()

    for i in range(BUFFERS - 1):
        begin(i)

    barrier = pltpu.get_barrier_semaphore()

    def greet(j, carry):
        pl.semaphore_signal(barrier, inc=1, device_id={"tensor": (t + 1 + j) % size}, device_id_type=MESH)
        return carry

    lax.fori_loop(0, size - 1, greet, 0)
    pl.semaphore_signal(barrier, inc=1, device_id={"context": other}, device_id_type=MESH)

    wide_in[...] = jnp.zeros_like(wide_in)
    wide_out[...] = jnp.zeros_like(wide_out)
    wide_in[:, :rank] = basis_in[...]
    wide_out[:, rank:] = basis_out[...]

    lanes = firsts.shape[2]
    lane = lax.broadcasted_iota(jnp.int32, (8, lanes), 1)

    def first(j, vector):
        return jnp.where(lane // (2 * slots) == j, ids[(j * rows) // block], vector)

    firsts[c] = lax.fori_loop(0, size, first, jnp.zeros((8, lanes), jnp.int32))
    pl.semaphore_wait(barrier, size)

    def share_firsts(index):
        return pltpu.make_async_remote_copy(
            src_ref=firsts.at[index], dst_ref=firsts.at[index], send_sem=first_send, recv_sem=first_recv,
            device_id={"context": other}, device_id_type=MESH,
        )

    share_firsts(c).start()

    def project(i):
        slot = i % BUFFERS
        for copy in load(i):
            copy.wait()

        @pl.when(i + BUFFERS - 1 < size)
        def _():
            begin(i + BUFFERS - 1)

        return jnp.dot(abuf[slot], wide_in[...], preferred_element_type=F32) + jnp.dot(
            gbuf[slot], wide_out[...], preferred_element_type=F32
        )

    def across(k):
        return pltpu.make_async_remote_copy(
            src_ref=sent.at[k], dst_ref=xbuf.at[k], send_sem=x_send.at[k], recv_sem=x_recv.at[k],
            device_id={"tensor": pair}, device_id_type=MESH,
        )

    def along(k, slot):
        return pltpu.make_async_remote_copy(
            src_ref=sent.at[half + k], dst_ref=zbuf.at[slot], send_sem=z_send.at[k], recv_sem=z_recv.at[slot],
            device_id={"tensor": 2 * k + parity}, device_id_type=MESH,
        )

    def first_half(i, carry):
        k = peer(i)
        sent[k] = project(i).astype(BF16)
        across(k).start()
        return carry

    lax.fori_loop(0, half, first_half, 0)

    def second_half(i, carry):
        k = peer(i)
        value = project(half + i)
        across(k).wait_recv()
        value = value + xbuf[k].astype(F32)
        acc[...] = value

        @pl.when(i < half - 1)
        def _():
            sent[half + k] = value.astype(BF16)
            along(k, mine).start()

        return carry

    lax.fori_loop(0, half, second_half, 0)

    def collect(j, carry):
        k = peer(j)
        along(k, k).wait_recv()
        acc[...] += zbuf[k].astype(F32)
        return carry

    lax.fori_loop(0, half - 1, collect, 0)

    proj = acc[...].astype(BF16)
    pick = one_hot(2 * rank, rank, lambda r, q: r == 2 * (q % (rank // 2)) + q // (rank // 2))
    twice = one_hot(2 * rank, 2 * rank, lambda r, q: r == rank + q % rank)
    left = jnp.dot(proj, pick, preferred_element_type=F32).astype(BF16)
    right = jnp.dot(proj, twice, preferred_element_type=F32).astype(BF16)
    deep = rank // 2
    part = min(block, rows)
    count = rows // part
    low = lax.broadcasted_iota(jnp.int32, (deep, 2 * rank), 1) < rank
    outers = []
    for k in range(count):
        o = lax.dot_general(
            left[k * part:(k + 1) * part], right[k * part:(k + 1) * part], (((0,), (0,)), ((), ())),
            preferred_element_type=F32,
        )
        outers.append(jnp.where(low, o[:deep], o[deep:]))
    start = (t * rows) // block
    offsets = [ids[start + k] - ids[start] for k in range(count)]
    for s in range(slots):
        total = jnp.zeros((deep, 2 * rank), F32)
        for k in range(count):
            total = total + outers[k] * jnp.where(offsets[k] == s, 1.0, 0.0)
        terms[s * deep:(s + 1) * deep, :] = total
    me = c * size + t
    width = deep // 2
    for a in range(width):
        value = jnp.concatenate(
            [terms[pl.ds(a, slots, stride=deep), :], terms[pl.ds(width + a, slots, stride=deep), :]], axis=0
        )
        held[me, :, a * 2 * rank:(a + 1) * 2 * rank] = value.astype(BF16)

    def give(index, send_sem, device):
        return pltpu.make_async_remote_copy(
            src_ref=held.at[index], dst_ref=held.at[index], send_sem=send_sem, recv_sem=g_recv.at[index],
            device_id=device, device_id_type=MESH,
        )

    def to_peer(k):
        return give(me, gz_send.at[k], {"tensor": 2 * k + parity})

    def to_pair(k):
        return give(c * size + 2 * k + parity, gx_send.at[k], {"tensor": pair})

    def to_core(k):
        return give(c * size + k, gc_send.at[k], {"context": other})

    def arrived(index):
        give(index, gc_send.at[0], {"context": other}).wait_recv()

    def loop(n, body):
        def step(j, carry):
            body(j)
            return carry

        lax.fori_loop(0, n, step, 0)

    loop(half - 1, lambda j: to_peer(peer(j)).start())
    to_pair(mine).start()
    to_core(t).start()

    def from_peer(j):
        k = peer(j)
        arrived(c * size + 2 * k + parity)
        to_pair(k).start()
        to_core(2 * k + parity).start()

    loop(half - 1, from_peer)

    def from_pair(j):
        k = 2 * peer(half - 1 + j) + 1 - parity
        arrived(c * size + k)
        to_core(k).start()

    loop(half, from_pair)
    share_firsts(other).wait_recv()
    loop(size, lambda k: arrived(other * size + k))

    wide = held.shape[2]
    chosen = []
    for core in range(2):
        row = lax.broadcasted_iota(jnp.int32, (2 * examples, lanes), 0)
        column = lax.broadcasted_iota(jnp.int32, (2 * examples, lanes), 1)
        at = firsts[core, 0:1, :] + column % slots
        hit = (row % examples == at) & (row // examples == column // slots % 2)
        chosen.append(jnp.where(hit, 1.0, 0.0).astype(BF16))
    tile = min(512, wide)
    for p in range(wide // tile):
        total = jnp.zeros((2 * examples, tile), F32)
        for core in range(2):
            data = held[core * size:(core + 1) * size, :, p * tile:(p + 1) * tile]
            total = total + jnp.dot(chosen[core], data.reshape(lanes, tile), preferred_element_type=F32)
        total = total.astype(BF16)
        sketches[:, p * tile:(p + 1) * tile] = total[:examples]
        sketches[:, wide + p * tile:wide + (p + 1) * tile] = total[examples:]

    local = lax.dot_general(
        val[...], sketches[...], (((1,), (1,)), ((), ())), preferred_element_type=F32
    )
    depth = pieces.shape[1]
    pieces[t] = jnp.concatenate([local[:depth], local[depth:]], axis=1)

    def send_scores(k, slot):
        return pltpu.make_async_remote_copy(
            src_ref=pieces.at[t], dst_ref=pieces.at[slot], send_sem=s_send.at[k], recv_sem=s_recv.at[slot],
            device_id={"tensor": k}, device_id_type=MESH,
        )

    loop(size - 1, lambda j: send_scores((t + 1 + j) % size, t).start())

    def got(j):
        k = (t + 1 + j) % size
        send_scores(k, k).wait_recv()

    loop(size - 1, got)
    table = pieces[...].reshape(size * depth, 2 * examples)
    result = jnp.zeros(scores.shape, F32)
    hots = [
        jnp.where(
            lax.broadcasted_iota(jnp.int32, (size * depth, scores.shape[1]), 0) // depth * (2 * depth)
            + h * depth
            + lax.broadcasted_iota(jnp.int32, (size * depth, scores.shape[1]), 0) % depth
            == owner[...],
            1.0, 0.0,
        ).astype(BF16)
        for h in range(2)
    ]
    for _ in range(3):
        digit = table.astype(BF16)
        table = table - digit.astype(F32)
        for h in range(2):
            result = result + lax.dot_general(
                digit[:, h * examples:(h + 1) * examples], hots[h], (((0,), (0,)), ((), ())),
                preferred_element_type=F32,
            )
    scores[...] = result

    share_firsts(c).wait_send()
    loop(half, lambda k: across(k).wait_send())
    loop(half - 1, lambda j: along(peer(j), mine).wait_send())
    loop(half - 1, lambda j: to_peer(peer(j)).wait_send())
    loop(half, lambda k: to_pair(k).wait_send())
    loop(size, lambda k: to_core(k).wait_send())
    loop(size - 1, lambda j: send_scores((t + 1 + j) % size, t).wait_send())


def per_device(activations, out_grads, basis_in, basis_out, val_sketches, val_owner, example_ids):
    size = lax.axis_size("tensor")
    tokens, deep_in = activations.shape
    deep_out = out_grads.shape[1]
    rank = basis_in.shape[1]
    nblock = example_ids.shape[0]
    examples = nblock * lax.axis_size("context") // 2
    rows = tokens // size
    half = size // 2
    slots = max(8, rows // (tokens // nblock))
    stored, width = val_sketches.shape
    depth = max(8, stored // 2)
    if 2 * depth != stored:
        val_sketches = jnp.pad(val_sketches, ((0, 2 * depth - stored), (0, 0)))
        val_owner_at = val_owner // stored * (2 * depth) + val_owner % stored
    else:
        val_owner_at = val_owner
    vmem = pl.BlockSpec(memory_space=pltpu.VMEM)
    hbm = pl.BlockSpec(memory_space=pl.ANY)
    dma = pltpu.SemaphoreType.DMA
    return pl.pallas_call(
        functools.partial(kernel, size, slots),
        out_shape=(
            jax.ShapeDtypeStruct((examples, width), BF16),
            jax.ShapeDtypeStruct((examples, stored), F32),
        ),
        in_specs=[hbm, hbm, vmem, vmem, vmem, vmem, pl.BlockSpec(memory_space=pltpu.SMEM)],
        out_specs=(vmem, vmem),
        scratch_shapes=[
            pltpu.VMEM((BUFFERS, rows, deep_in), BF16),
            pltpu.VMEM((BUFFERS, rows, deep_out), BF16),
            pltpu.VMEM((deep_in, 2 * rank), BF16),
            pltpu.VMEM((deep_out, 2 * rank), BF16),
            pltpu.VMEM((size, rows, 2 * rank), BF16),
            pltpu.VMEM((half, rows, 2 * rank), BF16),
            pltpu.VMEM((half, rows, 2 * rank), BF16),
            pltpu.VMEM((rows, 2 * rank), F32),
            pltpu.VMEM((slots * rank // 2, 2 * rank), F32),
            pltpu.VMEM((2, 8, size * 2 * slots), jnp.int32),
            pltpu.VMEM((2 * size, 2 * slots, width // 2), BF16),
            pltpu.VMEM((size, depth, 2 * examples), F32),
            dma((BUFFERS,)), dma((BUFFERS,)),
            dma((half,)), dma((half,)), dma((half,)), dma((half,)),
            dma, dma,
            dma((half,)), dma((half,)), dma((size,)), dma((2 * size,)),
            dma((size,)), dma((size,)),
        ],
        compiler_params=pltpu.CompilerParams(
            collective_id=0, has_side_effects=True, vmem_limit_bytes=48 * 1024 * 1024
        ),
        cost_estimate=pl.CostEstimate(
            flops=2 * tokens * (deep_in + deep_out) * rank,
            bytes_accessed=2 * tokens * (deep_in + deep_out),
            transcendentals=0,
        ),
    )(activations, out_grads, basis_in, basis_out, val_sketches, val_owner_at.reshape(1, stored), example_ids)


def solution(mesh):
    return jax.shard_map(
        per_device,
        mesh=mesh,
        in_specs=(
            P(("groups", "context"), "tensor"),
            P(("groups", "context"), "tensor"),
            P("tensor", None),
            P("tensor", None),
            P("tensor", None),
            P("tensor"),
            P(("groups", "context")),
        ),
        out_specs=(P("groups", None), P("groups", "tensor")),
        check_vma=False,
    )
```

```python
import functools

import jax
import jax.numpy as jnp
from jax import lax
from jax.experimental import pallas as pl
from jax.experimental.pallas import tpu as pltpu
from jax.sharding import PartitionSpec as P

MESH = pl.DeviceIdType.MESH
F32, BF16 = jnp.float32, jnp.bfloat16
BUFFERS = 3


def one_hot(rows, columns, hit):
    row = lax.broadcasted_iota(jnp.int32, (rows, columns), 0)
    column = lax.broadcasted_iota(jnp.int32, (rows, columns), 1)
    return jnp.where(hit(row, column), 1.0, 0.0).astype(BF16)


def kernel(
    size, slots, act, grads, basis_in, basis_out, val_hbm, owner_hbm, ids_hbm, sketches, scores,
    abuf, gbuf, val, owner, ids, wide_in, wide_out, sent, xbuf, zbuf, acc, terms, firsts, held, pieces,
    act_sem, grad_sem, in_sem, out_sem, val_sem, owner_sem, ids_sem, x_send, x_recv, z_send, z_recv, first_send, first_recv,
    gx_send, gz_send, gc_send, g_recv, s_send, s_recv,
):
    c = lax.axis_index("context")
    t = lax.axis_index("tensor")
    half = size // 2
    rows = acc.shape[0]
    rank = basis_in.shape[0]
    examples = sketches.shape[0]
    parity, mine = t % 2, t // 2
    pair = t + 1 - 2 * parity
    other = 1 - c
    nblock = ids.shape[0]
    block = rows * size // nblock

    def peer(j):
        flip, result, bit = half - 1 - j, 0, 1
        while bit < half:
            result = result + (mine // bit + flip // bit) % 2 * bit
            bit = bit * 2
        return result

    def near(i):
        return (i == size - 1) | ((i > 0) & (i % 2 == 0))

    def place(i):
        return jnp.where(i == size - 1, half - 1, jnp.where(near(i), (i + size - 2) // 2 % half, (i + 1) // 2))

    def target(i):
        return 2 * peer(place(i)) + jnp.where(near(i), parity, 1 - parity)

    def load(i):
        slot = i % BUFFERS
        start = pl.multiple_of(target(i) * rows, rows)
        return (
            pltpu.make_async_copy(act.at[pl.ds(start, rows), :], abuf.at[slot], act_sem.at[slot]),
            pltpu.make_async_copy(grads.at[pl.ds(start, rows), :], gbuf.at[slot], grad_sem.at[slot]),
        )

    def begin(i):
        for copy in load(i):
            copy.start()

    fixed = (
        pltpu.make_async_copy(basis_in, wide_in.at[:rank], in_sem),
        pltpu.make_async_copy(basis_out, wide_out.at[rank:], out_sem),
    )
    stored = (
        pltpu.make_async_copy(val_hbm, val, val_sem),
        pltpu.make_async_copy(owner_hbm, owner, owner_sem),
    )
    labels = pltpu.make_async_copy(ids_hbm, ids, ids_sem)
    labels.start()
    for copy in fixed:
        copy.start()
    for i in range(BUFFERS - 1):
        begin(i)

    barrier = pltpu.get_barrier_semaphore()

    def greet(j, carry):
        pl.semaphore_signal(barrier, inc=1, device_id={"tensor": (t + 1 + j) % size}, device_id_type=MESH)
        return carry

    lax.fori_loop(0, size - 1, greet, 0)
    pl.semaphore_signal(barrier, inc=1, device_id={"context": other}, device_id_type=MESH)

    wide_in[rank:] = jnp.zeros((rank, wide_in.shape[1]), BF16)
    wide_out[:rank] = jnp.zeros((rank, wide_out.shape[1]), BF16)

    labels.wait()
    lanes = firsts.shape[2]
    lane = lax.broadcasted_iota(jnp.int32, (8, lanes), 1)

    def first(j, vector):
        return jnp.where(lane // (2 * slots) == j, ids[(j * rows) // block], vector)

    firsts[c] = lax.fori_loop(0, size, first, jnp.zeros((8, lanes), jnp.int32))

    def share_firsts(index):
        return pltpu.make_async_remote_copy(
            src_ref=firsts.at[index], dst_ref=firsts.at[index], send_sem=first_send, recv_sem=first_recv,
            device_id={"context": other}, device_id_type=MESH,
        )

    for copy in fixed:
        copy.wait()
    turned = (((1,), (1,)), ((), ()))

    def project(i):
        slot = i % BUFFERS
        for copy in load(i):
            copy.wait()

        @pl.when(i + BUFFERS - 1 < size)
        def _():
            begin(i + BUFFERS - 1)

        return lax.dot_general(abuf[slot], wide_in[...], turned, preferred_element_type=F32) + lax.dot_general(
            gbuf[slot], wide_out[...], turned, preferred_element_type=F32
        )

    def across(k):
        return pltpu.make_async_remote_copy(
            src_ref=sent.at[k], dst_ref=xbuf.at[k], send_sem=x_send.at[k], recv_sem=x_recv.at[k],
            device_id={"tensor": pair}, device_id_type=MESH,
        )

    def along(k, slot):
        return pltpu.make_async_remote_copy(
            src_ref=sent.at[half + k], dst_ref=zbuf.at[slot], send_sem=z_send.at[k], recv_sem=z_recv.at[slot],
            device_id={"tensor": 2 * k + parity}, device_id_type=MESH,
        )

    def chunk(i, carry):
        k = peer(place(i))
        value = project(i)

        @pl.when(i == 0)
        def _():
            pl.semaphore_wait(barrier, size)
            share_firsts(c).start()

        @pl.when(jnp.logical_not(near(i)))
        def _():
            sent[k] = value.astype(BF16)
            across(k).start()

        @pl.when(near(i))
        def _():
            across(k).wait_recv()
            total = value + xbuf[k].astype(F32)
            acc[...] = total

            @pl.when(i < size - 1)
            def _():
                sent[half + k] = total.astype(BF16)
                along(k, mine).start()

        return carry

    lax.fori_loop(0, size, chunk, 0)
    for copy in stored:
        copy.start()

    def collect(j, carry):
        k = peer(j)
        along(k, k).wait_recv()
        acc[...] += zbuf[k].astype(F32)
        return carry

    lax.fori_loop(0, half - 1, collect, 0)

    proj = acc[...].astype(BF16)
    pick = one_hot(2 * rank, rank, lambda r, q: r == 2 * (q % (rank // 2)) + q // (rank // 2))
    twice = one_hot(2 * rank, 2 * rank, lambda r, q: r == rank + q % rank)
    left = jnp.dot(proj, pick, preferred_element_type=F32).astype(BF16)
    right = jnp.dot(proj, twice, preferred_element_type=F32).astype(BF16)
    deep = rank // 2
    part = min(block, rows)
    count = rows // part
    low = lax.broadcasted_iota(jnp.int32, (deep, 2 * rank), 1) < rank
    outers = []
    for k in range(count):
        o = lax.dot_general(
            left[k * part:(k + 1) * part], right[k * part:(k + 1) * part], (((0,), (0,)), ((), ())),
            preferred_element_type=F32,
        )
        outers.append(jnp.where(low, o[:deep], o[deep:]))
    start = (t * rows) // block
    offsets = [ids[start + k] - ids[start] for k in range(count)]
    for s in range(slots):
        total = jnp.zeros((deep, 2 * rank), F32)
        for k in range(count):
            total = total + outers[k] * jnp.where(offsets[k] == s, 1.0, 0.0)
        terms[s * deep:(s + 1) * deep, :] = total
    me = c * size + t
    width = deep // 2
    for a in range(width):
        value = jnp.concatenate(
            [terms[pl.ds(a, slots, stride=deep), :], terms[pl.ds(width + a, slots, stride=deep), :]], axis=0
        )
        held[me, :, a * 2 * rank:(a + 1) * 2 * rank] = value.astype(BF16)

    def give(index, send_sem, device):
        return pltpu.make_async_remote_copy(
            src_ref=held.at[index], dst_ref=held.at[index], send_sem=send_sem, recv_sem=g_recv.at[index],
            device_id=device, device_id_type=MESH,
        )

    def to_peer(k):
        return give(me, gz_send.at[k], {"tensor": 2 * k + parity})

    def to_pair(k):
        return give(c * size + 2 * k + parity, gx_send.at[k], {"tensor": pair})

    def to_core(k):
        return give(c * size + k, gc_send.at[k], {"context": other})

    def arrived(index):
        give(index, gc_send.at[0], {"context": other}).wait_recv()

    def loop(n, body):
        def step(j, carry):
            body(j)
            return carry

        lax.fori_loop(0, n, step, 0)

    loop(half - 1, lambda j: to_peer(peer(j)).start())
    to_pair(mine).start()
    to_core(t).start()

    def from_peer(j):
        k = peer(j)
        arrived(c * size + 2 * k + parity)
        to_pair(k).start()
        to_core(2 * k + parity).start()

    loop(half - 1, from_peer)

    def from_pair(j):
        k = 2 * peer(half - 1 + j) + 1 - parity
        arrived(c * size + k)
        to_core(k).start()

    loop(half, from_pair)
    share_firsts(other).wait_recv()
    loop(size, lambda k: arrived(other * size + k))

    wide = held.shape[2]
    chosen = []
    for core in range(2):
        row = lax.broadcasted_iota(jnp.int32, (2 * examples, lanes), 0)
        column = lax.broadcasted_iota(jnp.int32, (2 * examples, lanes), 1)
        at = firsts[core, 0:1, :] + column % slots
        hit = (row % examples == at) & (row // examples == column // slots % 2)
        chosen.append(jnp.where(hit, 1.0, 0.0).astype(BF16))
    tile = min(512, wide)
    for p in range(wide // tile):
        total = jnp.zeros((2 * examples, tile), F32)
        for core in range(2):
            data = held[core * size:(core + 1) * size, :, p * tile:(p + 1) * tile]
            total = total + jnp.dot(chosen[core], data.reshape(lanes, tile), preferred_element_type=F32)
        total = total.astype(BF16)
        sketches[:, p * tile:(p + 1) * tile] = total[:examples]
        sketches[:, wide + p * tile:wide + (p + 1) * tile] = total[examples:]

    for copy in stored:
        copy.wait()
    local = lax.dot_general(val[...], sketches[...], turned, preferred_element_type=F32)
    depth = pieces.shape[1]
    pieces[t] = jnp.concatenate([local[:depth], local[depth:]], axis=1)

    def send_scores(k, slot):
        return pltpu.make_async_remote_copy(
            src_ref=pieces.at[t], dst_ref=pieces.at[slot], send_sem=s_send.at[k], recv_sem=s_recv.at[slot],
            device_id={"tensor": k}, device_id_type=MESH,
        )

    loop(size - 1, lambda j: send_scores((t + 1 + j) % size, t).start())

    def got(j):
        k = (t + 1 + j) % size
        send_scores(k, k).wait_recv()

    loop(size - 1, got)
    table = pieces[...].reshape(size * depth, 2 * examples)
    result = jnp.zeros(scores.shape, F32)
    hots = [
        jnp.where(
            lax.broadcasted_iota(jnp.int32, (size * depth, scores.shape[1]), 0) // depth * (2 * depth)
            + h * depth
            + lax.broadcasted_iota(jnp.int32, (size * depth, scores.shape[1]), 0) % depth
            == owner[...],
            1.0, 0.0,
        ).astype(BF16)
        for h in range(2)
    ]
    for _ in range(3):
        digit = table.astype(BF16)
        table = table - digit.astype(F32)
        for h in range(2):
            result = result + lax.dot_general(
                digit[:, h * examples:(h + 1) * examples], hots[h], (((0,), (0,)), ((), ())),
                preferred_element_type=F32,
            )
    scores[...] = result

    share_firsts(c).wait_send()
    loop(half, lambda k: across(k).wait_send())
    loop(half - 1, lambda j: along(peer(j), mine).wait_send())
    loop(half - 1, lambda j: to_peer(peer(j)).wait_send())
    loop(half, lambda k: to_pair(k).wait_send())
    loop(size, lambda k: to_core(k).wait_send())
    loop(size - 1, lambda j: send_scores((t + 1 + j) % size, t).wait_send())


def per_device(activations, out_grads, basis_in, basis_out, val_sketches, val_owner, example_ids):
    size = lax.axis_size("tensor")
    tokens, deep_in = activations.shape
    deep_out = out_grads.shape[1]
    rank = basis_in.shape[1]
    nblock = example_ids.shape[0]
    examples = nblock * lax.axis_size("context") // 2
    rows = tokens // size
    half = size // 2
    slots = max(8, rows // (tokens // nblock))
    stored, width = val_sketches.shape
    depth = max(8, stored // 2)
    if 2 * depth != stored:
        val_sketches = jnp.pad(val_sketches, ((0, 2 * depth - stored), (0, 0)))
        val_owner_at = val_owner // stored * (2 * depth) + val_owner % stored
    else:
        val_owner_at = val_owner
    vmem = pl.BlockSpec(memory_space=pltpu.VMEM)
    hbm = pl.BlockSpec(memory_space=pltpu.HBM)
    dma = pltpu.SemaphoreType.DMA
    return pl.pallas_call(
        functools.partial(kernel, size, slots),
        out_shape=(
            jax.ShapeDtypeStruct((examples, width), BF16),
            jax.ShapeDtypeStruct((examples, stored), F32),
        ),
        in_specs=[hbm] * 7,
        out_specs=(vmem, vmem),
        scratch_shapes=[
            pltpu.VMEM((BUFFERS, rows, deep_in), BF16),
            pltpu.VMEM((BUFFERS, rows, deep_out), BF16),
            pltpu.VMEM((2 * depth, width), BF16),
            pltpu.VMEM((1, stored), jnp.int32),
            pltpu.SMEM((nblock,), jnp.int32),
            pltpu.VMEM((2 * rank, deep_in), BF16),
            pltpu.VMEM((2 * rank, deep_out), BF16),
            pltpu.VMEM((size, rows, 2 * rank), BF16),
            pltpu.VMEM((half, rows, 2 * rank), BF16),
            pltpu.VMEM((half, rows, 2 * rank), BF16),
            pltpu.VMEM((rows, 2 * rank), F32),
            pltpu.VMEM((slots * rank // 2, 2 * rank), F32),
            pltpu.VMEM((2, 8, size * 2 * slots), jnp.int32),
            pltpu.VMEM((2 * size, 2 * slots, width // 2), BF16),
            pltpu.VMEM((size, depth, 2 * examples), F32),
            dma((BUFFERS,)), dma((BUFFERS,)), dma, dma, dma, dma, dma,
            dma((half,)), dma((half,)), dma((half,)), dma((half,)),
            dma, dma,
            dma((half,)), dma((half,)), dma((size,)), dma((2 * size,)),
            dma((size,)), dma((size,)),
        ],
        compiler_params=pltpu.CompilerParams(
            collective_id=0, has_side_effects=True, vmem_limit_bytes=48 * 1024 * 1024
        ),
        cost_estimate=pl.CostEstimate(
            flops=2 * tokens * (deep_in + deep_out) * rank,
            bytes_accessed=2 * tokens * (deep_in + deep_out),
            transcendentals=0,
        ),
    )(*[pltpu.with_memory_space_constraint(x, pltpu.HBM) for x in (activations, out_grads, basis_in.T, basis_out.T, val_sketches, val_owner_at.reshape(1, stored), example_ids)])


def solution(mesh):
    return jax.shard_map(
        per_device,
        mesh=mesh,
        in_specs=(
            P(("groups", "context"), "tensor"),
            P(("groups", "context"), "tensor"),
            P("tensor", None),
            P("tensor", None),
            P("tensor", None),
            P("tensor"),
            P(("groups", "context")),
        ),
        out_specs=(P("groups", None), P("groups", "tensor")),
        check_vma=False,
    )
```

```python
import functools

import jax
import jax.numpy as jnp
from jax import lax
from jax.experimental import pallas as pl
from jax.experimental.pallas import tpu as pltpu
from jax.sharding import PartitionSpec as P

MESH = pl.DeviceIdType.MESH
F32, BF16 = jnp.float32, jnp.bfloat16
BUFFERS = 3


def one_hot(rows, columns, hit):
    row = lax.broadcasted_iota(jnp.int32, (rows, columns), 0)
    column = lax.broadcasted_iota(jnp.int32, (rows, columns), 1)
    return jnp.where(hit(row, column), 1.0, 0.0).astype(BF16)


def kernel(
    size, slots, act, grads, basis_in, basis_out, val_hbm, owner_hbm, ids_hbm, sketches, scores,
    abuf, gbuf, val, owner, ids, wide_in, wide_out, sent, xbuf, zbuf, acc, terms, firsts, held, pieces,
    act_sem, grad_sem, in_sem, out_sem, val_sem, owner_sem, ids_sem, x_send, x_recv, z_send, z_recv, first_send, first_recv,
    gx_send, gz_send, gc_send, g_recv, s_send, s_recv,
):
    c = lax.axis_index("context")
    t = lax.axis_index("tensor")
    half = size // 2
    rows = acc.shape[0]
    rank = basis_in.shape[0]
    examples = sketches.shape[0]
    parity, mine = t % 2, t // 2
    pair = t + 1 - 2 * parity
    other = 1 - c
    nblock = ids.shape[0]
    block = rows * size // nblock

    def peer(j):
        flip, result, bit = half - 1 - j, 0, 1
        while bit < half:
            result = result + (mine // bit + flip // bit) % 2 * bit
            bit = bit * 2
        return result

    def near(i):
        return (i == size - 1) | ((i > 0) & (i % 2 == 0))

    def place(i):
        return jnp.where(i == size - 1, half - 1, jnp.where(near(i), (i + size - 2) // 2 % half, (i + 1) // 2))

    def target(i):
        return 2 * peer(place(i)) + jnp.where(near(i), parity, 1 - parity)

    def load(i):
        slot = i % BUFFERS
        start = pl.multiple_of(target(i) * rows, rows)
        return (
            pltpu.make_async_copy(act.at[pl.ds(start, rows), :], abuf.at[slot], act_sem.at[slot]),
            pltpu.make_async_copy(grads.at[pl.ds(start, rows), :], gbuf.at[slot], grad_sem.at[slot]),
        )

    def begin(i):
        for copy in load(i):
            copy.start()

    fixed = (
        pltpu.make_async_copy(basis_in, wide_in.at[:rank], in_sem),
        pltpu.make_async_copy(basis_out, wide_out.at[rank:], out_sem),
    )
    stored = (
        pltpu.make_async_copy(val_hbm, val, val_sem),
        pltpu.make_async_copy(owner_hbm, owner, owner_sem),
    )
    labels = pltpu.make_async_copy(ids_hbm, ids, ids_sem)
    labels.start()
    for copy in fixed:
        copy.start()
    for i in range(BUFFERS - 1):
        begin(i)

    barrier = pltpu.get_barrier_semaphore()

    def greet(j, carry):
        pl.semaphore_signal(barrier, inc=1, device_id={"tensor": (t + 1 + j) % size}, device_id_type=MESH)
        return carry

    lax.fori_loop(0, size - 1, greet, 0)
    pl.semaphore_signal(barrier, inc=1, device_id={"context": other}, device_id_type=MESH)

    wide_in[rank:] = jnp.zeros((rank, wide_in.shape[1]), BF16)
    wide_out[:rank] = jnp.zeros((rank, wide_out.shape[1]), BF16)

    labels.wait()
    lanes = firsts.shape[2]
    lane = lax.broadcasted_iota(jnp.int32, (8, lanes), 1)

    def first(j, vector):
        return jnp.where(lane // (2 * slots) == j, ids[(j * rows) // block], vector)

    firsts[c] = lax.fori_loop(0, size, first, jnp.zeros((8, lanes), jnp.int32))

    def share_firsts(index):
        return pltpu.make_async_remote_copy(
            src_ref=firsts.at[index], dst_ref=firsts.at[index], send_sem=first_send, recv_sem=first_recv,
            device_id={"context": other}, device_id_type=MESH,
        )

    for copy in fixed:
        copy.wait()
    turned = (((1,), (1,)), ((), ()))

    def project(i):
        slot = i % BUFFERS
        for copy in load(i):
            copy.wait()

        @pl.when(i + BUFFERS - 1 < size)
        def _():
            begin(i + BUFFERS - 1)

        return lax.dot_general(abuf[slot], wide_in[...], turned, preferred_element_type=F32) + lax.dot_general(
            gbuf[slot], wide_out[...], turned, preferred_element_type=F32
        )

    def across(k):
        return pltpu.make_async_remote_copy(
            src_ref=sent.at[k], dst_ref=xbuf.at[k], send_sem=x_send.at[k], recv_sem=x_recv.at[k],
            device_id={"tensor": pair}, device_id_type=MESH,
        )

    def along(k, slot):
        return pltpu.make_async_remote_copy(
            src_ref=sent.at[half + k], dst_ref=zbuf.at[slot], send_sem=z_send.at[k], recv_sem=z_recv.at[slot],
            device_id={"tensor": 2 * k + parity}, device_id_type=MESH,
        )

    def chunk(i, carry):
        k = peer(place(i))
        value = project(i)

        @pl.when(i == 0)
        def _():
            pl.semaphore_wait(barrier, size)
            share_firsts(c).start()

        @pl.when(jnp.logical_not(near(i)))
        def _():
            sent[k] = value.astype(BF16)
            across(k).start()

        @pl.when(near(i))
        def _():
            across(k).wait_recv()
            total = value + xbuf[k].astype(F32)
            acc[...] = total

            @pl.when(i < size - 1)
            def _():
                sent[half + k] = total.astype(BF16)
                along(k, mine).start()

        return carry

    lax.fori_loop(0, size, chunk, 0)
    for copy in stored:
        copy.start()

    def collect(j, carry):
        k = peer(j)
        along(k, k).wait_recv()
        acc[...] += zbuf[k].astype(F32)
        return carry

    lax.fori_loop(0, half - 1, collect, 0)

    proj = acc[...].astype(BF16)
    pick = one_hot(2 * rank, rank, lambda r, q: r == 2 * (q % (rank // 2)) + q // (rank // 2))
    twice = one_hot(2 * rank, 2 * rank, lambda r, q: r == rank + q % rank)
    left = jnp.dot(proj, pick, preferred_element_type=F32).astype(BF16)
    right = jnp.dot(proj, twice, preferred_element_type=F32).astype(BF16)
    deep = rank // 2
    part = min(block, rows)
    count = rows // part
    low = lax.broadcasted_iota(jnp.int32, (deep, 2 * rank), 1) < rank
    outers = []
    for k in range(count):
        o = lax.dot_general(
            left[k * part:(k + 1) * part], right[k * part:(k + 1) * part], (((0,), (0,)), ((), ())),
            preferred_element_type=F32,
        )
        outers.append(jnp.where(low, o[:deep], o[deep:]))
    start = (t * rows) // block
    offsets = [ids[start + k] - ids[start] for k in range(count)]
    for s in range(slots):
        total = jnp.zeros((deep, 2 * rank), F32)
        for k in range(count):
            total = total + outers[k] * jnp.where(offsets[k] == s, 1.0, 0.0)
        terms[s * deep:(s + 1) * deep, :] = total
    me = c * size + t
    width = deep // 2
    for a in range(width):
        value = jnp.concatenate(
            [terms[pl.ds(a, slots, stride=deep), :], terms[pl.ds(width + a, slots, stride=deep), :]], axis=0
        )
        held[me, :, a * 2 * rank:(a + 1) * 2 * rank] = value.astype(BF16)

    def give(index, send_sem, device):
        return pltpu.make_async_remote_copy(
            src_ref=held.at[index], dst_ref=held.at[index], send_sem=send_sem, recv_sem=g_recv.at[index],
            device_id=device, device_id_type=MESH,
        )

    def to_peer(k):
        return give(me, gz_send.at[k], {"tensor": 2 * k + parity})

    def to_pair(k):
        return give(c * size + 2 * k + parity, gx_send.at[k], {"tensor": pair})

    def to_diagonal():
        return give(me, gx_send.at[peer(half - 2)], {"tensor": 2 * peer(half - 2) + 1 - parity})

    def to_core(k):
        return give(c * size + k, gc_send.at[k], {"context": other})

    def arrived(index):
        give(index, gc_send.at[0], {"context": other}).wait_recv()

    def loop(n, body):
        def step(j, carry):
            body(j)
            return carry

        lax.fori_loop(0, n, step, 0)

    loop(half - 1, lambda j: to_peer(peer(j)).start())
    to_pair(mine).start()
    if half > 1:
        to_diagonal().start()
    to_core(t).start()

    def from_peer(j):
        k = peer(j)
        arrived(c * size + 2 * k + parity)

        @pl.when(j < half - 2)
        def _():
            to_pair(k).start()

        to_core(2 * k + parity).start()

    loop(half - 1, from_peer)

    def from_pair(j):
        k = 2 * peer((half - 1 + j) % half) + 1 - parity
        arrived(c * size + k)
        to_core(k).start()

    loop(half, from_pair)
    share_firsts(other).wait_recv()
    loop(size, lambda k: arrived(other * size + k))

    wide = held.shape[2]
    chosen = []
    for core in range(2):
        row = lax.broadcasted_iota(jnp.int32, (2 * examples, lanes), 0)
        column = lax.broadcasted_iota(jnp.int32, (2 * examples, lanes), 1)
        at = firsts[core, 0:1, :] + column % slots
        hit = (row % examples == at) & (row // examples == column // slots % 2)
        chosen.append(jnp.where(hit, 1.0, 0.0).astype(BF16))
    tile = min(512, wide)
    for p in range(wide // tile):
        total = jnp.zeros((2 * examples, tile), F32)
        for core in range(2):
            data = held[core * size:(core + 1) * size, :, p * tile:(p + 1) * tile]
            total = total + jnp.dot(chosen[core], data.reshape(lanes, tile), preferred_element_type=F32)
        total = total.astype(BF16)
        sketches[:, p * tile:(p + 1) * tile] = total[:examples]
        sketches[:, wide + p * tile:wide + (p + 1) * tile] = total[examples:]

    for copy in stored:
        copy.wait()
    local = lax.dot_general(val[...], sketches[...], turned, preferred_element_type=F32)
    depth = pieces.shape[1]
    pieces[t] = jnp.concatenate([local[:depth], local[depth:]], axis=1)

    def send_scores(k, slot):
        return pltpu.make_async_remote_copy(
            src_ref=pieces.at[t], dst_ref=pieces.at[slot], send_sem=s_send.at[k], recv_sem=s_recv.at[slot],
            device_id={"tensor": k}, device_id_type=MESH,
        )

    loop(size - 1, lambda j: send_scores((t + 1 + j) % size, t).start())

    def got(j):
        k = (t + 1 + j) % size
        send_scores(k, k).wait_recv()

    loop(size - 1, got)
    table = pieces[...].reshape(size * depth, 2 * examples)
    result = jnp.zeros(scores.shape, F32)
    hots = [
        jnp.where(
            lax.broadcasted_iota(jnp.int32, (size * depth, scores.shape[1]), 0) // depth * (2 * depth)
            + h * depth
            + lax.broadcasted_iota(jnp.int32, (size * depth, scores.shape[1]), 0) % depth
            == owner[...],
            1.0, 0.0,
        ).astype(BF16)
        for h in range(2)
    ]
    for _ in range(3):
        digit = table.astype(BF16)
        table = table - digit.astype(F32)
        for h in range(2):
            result = result + lax.dot_general(
                digit[:, h * examples:(h + 1) * examples], hots[h], (((0,), (0,)), ((), ())),
                preferred_element_type=F32,
            )
    scores[...] = result

    share_firsts(c).wait_send()
    loop(half, lambda k: across(k).wait_send())
    loop(half - 1, lambda j: along(peer(j), mine).wait_send())
    loop(half - 1, lambda j: to_peer(peer(j)).wait_send())
    loop(half - 2, lambda j: to_pair(peer(j)).wait_send())
    to_pair(mine).wait_send()
    if half > 1:
        to_diagonal().wait_send()
    loop(size, lambda k: to_core(k).wait_send())
    loop(size - 1, lambda j: send_scores((t + 1 + j) % size, t).wait_send())


def per_device(activations, out_grads, basis_in, basis_out, val_sketches, val_owner, example_ids):
    size = lax.axis_size("tensor")
    tokens, deep_in = activations.shape
    deep_out = out_grads.shape[1]
    rank = basis_in.shape[1]
    nblock = example_ids.shape[0]
    examples = nblock * lax.axis_size("context") // 2
    rows = tokens // size
    half = size // 2
    slots = max(8, rows // (tokens // nblock))
    stored, width = val_sketches.shape
    depth = max(8, stored // 2)
    if 2 * depth != stored:
        val_sketches = jnp.pad(val_sketches, ((0, 2 * depth - stored), (0, 0)))
        val_owner_at = val_owner // stored * (2 * depth) + val_owner % stored
    else:
        val_owner_at = val_owner
    vmem = pl.BlockSpec(memory_space=pltpu.VMEM)
    hbm = pl.BlockSpec(memory_space=pltpu.HBM)
    dma = pltpu.SemaphoreType.DMA
    return pl.pallas_call(
        functools.partial(kernel, size, slots),
        out_shape=(
            jax.ShapeDtypeStruct((examples, width), BF16),
            jax.ShapeDtypeStruct((examples, stored), F32),
        ),
        in_specs=[hbm] * 7,
        out_specs=(vmem, vmem),
        scratch_shapes=[
            pltpu.VMEM((BUFFERS, rows, deep_in), BF16),
            pltpu.VMEM((BUFFERS, rows, deep_out), BF16),
            pltpu.VMEM((2 * depth, width), BF16),
            pltpu.VMEM((1, stored), jnp.int32),
            pltpu.SMEM((nblock,), jnp.int32),
            pltpu.VMEM((2 * rank, deep_in), BF16),
            pltpu.VMEM((2 * rank, deep_out), BF16),
            pltpu.VMEM((size, rows, 2 * rank), BF16),
            pltpu.VMEM((half, rows, 2 * rank), BF16),
            pltpu.VMEM((half, rows, 2 * rank), BF16),
            pltpu.VMEM((rows, 2 * rank), F32),
            pltpu.VMEM((slots * rank // 2, 2 * rank), F32),
            pltpu.VMEM((2, 8, size * 2 * slots), jnp.int32),
            pltpu.VMEM((2 * size, 2 * slots, width // 2), BF16),
            pltpu.VMEM((size, depth, 2 * examples), F32),
            dma((BUFFERS,)), dma((BUFFERS,)), dma, dma, dma, dma, dma,
            dma((half,)), dma((half,)), dma((half,)), dma((half,)),
            dma, dma,
            dma((half,)), dma((half,)), dma((size,)), dma((2 * size,)),
            dma((size,)), dma((size,)),
        ],
        compiler_params=pltpu.CompilerParams(
            collective_id=0, has_side_effects=True, vmem_limit_bytes=48 * 1024 * 1024
        ),
        cost_estimate=pl.CostEstimate(
            flops=2 * tokens * (deep_in + deep_out) * rank,
            bytes_accessed=2 * tokens * (deep_in + deep_out),
            transcendentals=0,
        ),
    )(*[pltpu.with_memory_space_constraint(x, pltpu.HBM) for x in (activations, out_grads, basis_in.T, basis_out.T, val_sketches, val_owner_at.reshape(1, stored), example_ids)])


def solution(mesh):
    return jax.shard_map(
        per_device,
        mesh=mesh,
        in_specs=(
            P(("groups", "context"), "tensor"),
            P(("groups", "context"), "tensor"),
            P("tensor", None),
            P("tensor", None),
            P("tensor", None),
            P("tensor"),
            P(("groups", "context")),
        ),
        out_specs=(P("groups", None), P("groups", "tensor")),
        check_vma=False,
    )
```

```python
import functools

import jax
import jax.numpy as jnp
from jax import lax
from jax.experimental import pallas as pl
from jax.experimental.pallas import tpu as pltpu
from jax.sharding import PartitionSpec as P

MESH = pl.DeviceIdType.MESH
F32, BF16 = jnp.float32, jnp.bfloat16
BUFFERS = 3


def one_hot(rows, columns, hit):
    row = lax.broadcasted_iota(jnp.int32, (rows, columns), 0)
    column = lax.broadcasted_iota(jnp.int32, (rows, columns), 1)
    return jnp.where(hit(row, column), 1.0, 0.0).astype(BF16)


def kernel(
    size, slots, act, grads, basis_in, basis_out, val_hbm, owner_hbm, ids_hbm, sketches, scores,
    abuf, gbuf, val, owner, ids, wide_in, wide_out, sent, xbuf, zbuf, acc, terms, firsts, held, pieces,
    act_sem, grad_sem, in_sem, out_sem, val_sem, owner_sem, ids_sem, x_send, x_recv, z_send, z_recv, first_send, first_recv,
    gx_send, gz_send, gc_send, g_recv, s_send, s_recv,
):
    c = lax.axis_index("context")
    t = lax.axis_index("tensor")
    half = size // 2
    rows = acc.shape[0]
    rank = basis_in.shape[0]
    examples = sketches.shape[0]
    parity, mine = t % 2, t // 2
    pair = t + 1 - 2 * parity
    other = 1 - c
    nblock = ids.shape[0]
    block = rows * size // nblock

    def peer(j):
        flip, result, bit = half - 1 - j, 0, 1
        while bit < half:
            result = result + (mine // bit + flip // bit) % 2 * bit
            bit = bit * 2
        return result

    def near(i):
        return (i >= size - 2) | ((i >= 3) & (i % 2 == 1))

    def place(i):
        return jnp.where(i >= size - 2, i - half, jnp.where(near(i), (i - 3) // 2 % half, jnp.where(i < 2, i, i // 2 + 1)))

    def target(i):
        return 2 * peer(place(i)) + jnp.where(near(i), parity, 1 - parity)

    def load(i):
        slot = i % BUFFERS
        start = pl.multiple_of(target(i) * rows, rows)
        return (
            pltpu.make_async_copy(act.at[pl.ds(start, rows), :], abuf.at[slot], act_sem.at[slot]),
            pltpu.make_async_copy(grads.at[pl.ds(start, rows), :], gbuf.at[slot], grad_sem.at[slot]),
        )

    def begin(i):
        for copy in load(i):
            copy.start()

    fixed = (
        pltpu.make_async_copy(basis_in, wide_in.at[:rank], in_sem),
        pltpu.make_async_copy(basis_out, wide_out.at[rank:], out_sem),
    )
    stored = (
        pltpu.make_async_copy(val_hbm, val, val_sem),
        pltpu.make_async_copy(owner_hbm, owner, owner_sem),
    )
    labels = pltpu.make_async_copy(ids_hbm, ids, ids_sem)
    labels.start()
    for copy in fixed:
        copy.start()
    for i in range(BUFFERS - 1):
        begin(i)

    barrier = pltpu.get_barrier_semaphore()

    def greet(j, carry):
        pl.semaphore_signal(barrier, inc=1, device_id={"tensor": (t + 1 + j) % size}, device_id_type=MESH)
        return carry

    lax.fori_loop(0, size - 1, greet, 0)
    pl.semaphore_signal(barrier, inc=1, device_id={"context": other}, device_id_type=MESH)

    wide_in[rank:] = jnp.zeros((rank, wide_in.shape[1]), BF16)
    wide_out[:rank] = jnp.zeros((rank, wide_out.shape[1]), BF16)

    labels.wait()
    lanes = firsts.shape[2]
    lane = lax.broadcasted_iota(jnp.int32, (8, lanes), 1)

    def first(j, vector):
        return jnp.where(lane // (2 * slots) == j, ids[(j * rows) // block], vector)

    firsts[c] = lax.fori_loop(0, size, first, jnp.zeros((8, lanes), jnp.int32))

    def share_firsts(index):
        return pltpu.make_async_remote_copy(
            src_ref=firsts.at[index], dst_ref=firsts.at[index], send_sem=first_send, recv_sem=first_recv,
            device_id={"context": other}, device_id_type=MESH,
        )

    for copy in fixed:
        copy.wait()
    turned = (((1,), (1,)), ((), ()))

    def project(i):
        slot = i % BUFFERS
        for copy in load(i):
            copy.wait()

        @pl.when(i + BUFFERS - 1 < size)
        def _():
            begin(i + BUFFERS - 1)

        return lax.dot_general(abuf[slot], wide_in[...], turned, preferred_element_type=F32) + lax.dot_general(
            gbuf[slot], wide_out[...], turned, preferred_element_type=F32
        )

    def across(k):
        return pltpu.make_async_remote_copy(
            src_ref=sent.at[k], dst_ref=xbuf.at[k], send_sem=x_send.at[k], recv_sem=x_recv.at[k],
            device_id={"tensor": pair}, device_id_type=MESH,
        )

    def along(k, slot):
        return pltpu.make_async_remote_copy(
            src_ref=sent.at[half + k], dst_ref=zbuf.at[slot], send_sem=z_send.at[k], recv_sem=z_recv.at[slot],
            device_id={"tensor": 2 * k + parity}, device_id_type=MESH,
        )

    def chunk(i, carry):
        k = peer(place(i))
        value = project(i)

        @pl.when(i == 0)
        def _():
            pl.semaphore_wait(barrier, size)
            share_firsts(c).start()

        @pl.when(jnp.logical_not(near(i)))
        def _():
            sent[k] = value.astype(BF16)
            across(k).start()

        @pl.when(near(i))
        def _():
            across(k).wait_recv()
            total = value + xbuf[k].astype(F32)
            acc[...] = total

            @pl.when(i < size - 1)
            def _():
                sent[half + k] = total.astype(BF16)
                along(k, mine).start()

        return carry

    lax.fori_loop(0, size, chunk, 0)
    for copy in stored:
        copy.start()

    def collect(j, carry):
        k = peer(j)
        along(k, k).wait_recv()
        acc[...] += zbuf[k].astype(F32)
        return carry

    lax.fori_loop(0, half - 1, collect, 0)

    proj = acc[...].astype(BF16)
    pick = one_hot(2 * rank, rank, lambda r, q: r == 2 * (q % (rank // 2)) + q // (rank // 2))
    twice = one_hot(2 * rank, 2 * rank, lambda r, q: r == rank + q % rank)
    left = jnp.dot(proj, pick, preferred_element_type=F32).astype(BF16)
    right = jnp.dot(proj, twice, preferred_element_type=F32).astype(BF16)
    deep = rank // 2
    part = min(block, rows)
    count = rows // part
    low = lax.broadcasted_iota(jnp.int32, (deep, 2 * rank), 1) < rank
    outers = []
    for k in range(count):
        o = lax.dot_general(
            left[k * part:(k + 1) * part], right[k * part:(k + 1) * part], (((0,), (0,)), ((), ())),
            preferred_element_type=F32,
        )
        outers.append(jnp.where(low, o[:deep], o[deep:]))
    start = (t * rows) // block
    offsets = [ids[start + k] - ids[start] for k in range(count)]
    for s in range(slots):
        total = jnp.zeros((deep, 2 * rank), F32)
        for k in range(count):
            total = total + outers[k] * jnp.where(offsets[k] == s, 1.0, 0.0)
        terms[s * deep:(s + 1) * deep, :] = total
    me = c * size + t
    width = deep // 2
    for a in range(width):
        value = jnp.concatenate(
            [terms[pl.ds(a, slots, stride=deep), :], terms[pl.ds(width + a, slots, stride=deep), :]], axis=0
        )
        held[me, :, a * 2 * rank:(a + 1) * 2 * rank] = value.astype(BF16)

    def give(index, send_sem, device):
        return pltpu.make_async_remote_copy(
            src_ref=held.at[index], dst_ref=held.at[index], send_sem=send_sem, recv_sem=g_recv.at[index],
            device_id=device, device_id_type=MESH,
        )

    def to_peer(k):
        return give(me, gz_send.at[k], {"tensor": 2 * k + parity})

    def to_pair(k):
        return give(c * size + 2 * k + parity, gx_send.at[k], {"tensor": pair})

    def to_diagonal():
        return give(me, gx_send.at[peer(half - 2)], {"tensor": 2 * peer(half - 2) + 1 - parity})

    def to_core(k):
        return give(c * size + k, gc_send.at[k], {"context": other})

    def arrived(index):
        give(index, gc_send.at[0], {"context": other}).wait_recv()

    def loop(n, body):
        def step(j, carry):
            body(j)
            return carry

        lax.fori_loop(0, n, step, 0)

    loop(half - 1, lambda j: to_peer(peer(j)).start())
    to_pair(mine).start()
    if half > 1:
        to_diagonal().start()
    to_core(t).start()

    def from_peer(j):
        k = peer(j)
        arrived(c * size + 2 * k + parity)

        @pl.when(j < half - 2)
        def _():
            to_pair(k).start()

        to_core(2 * k + parity).start()

    loop(half - 1, from_peer)

    def from_pair(j):
        k = 2 * peer((half - 1 + j) % half) + 1 - parity
        arrived(c * size + k)
        to_core(k).start()

    loop(half, from_pair)
    share_firsts(other).wait_recv()
    loop(size, lambda k: arrived(other * size + k))

    wide = held.shape[2]
    chosen = []
    for core in range(2):
        row = lax.broadcasted_iota(jnp.int32, (2 * examples, lanes), 0)
        column = lax.broadcasted_iota(jnp.int32, (2 * examples, lanes), 1)
        at = firsts[core, 0:1, :] + column % slots
        hit = (row % examples == at) & (row // examples == column // slots % 2)
        chosen.append(jnp.where(hit, 1.0, 0.0).astype(BF16))
    tile = min(512, wide)
    for p in range(wide // tile):
        total = jnp.zeros((2 * examples, tile), F32)
        for core in range(2):
            data = held[core * size:(core + 1) * size, :, p * tile:(p + 1) * tile]
            total = total + jnp.dot(chosen[core], data.reshape(lanes, tile), preferred_element_type=F32)
        total = total.astype(BF16)
        sketches[:, p * tile:(p + 1) * tile] = total[:examples]
        sketches[:, wide + p * tile:wide + (p + 1) * tile] = total[examples:]

    for copy in stored:
        copy.wait()
    local = lax.dot_general(val[...], sketches[...], turned, preferred_element_type=F32)
    depth = pieces.shape[1]
    pieces[t] = jnp.concatenate([local[:depth], local[depth:]], axis=1)

    def send_scores(k, slot):
        return pltpu.make_async_remote_copy(
            src_ref=pieces.at[t], dst_ref=pieces.at[slot], send_sem=s_send.at[k], recv_sem=s_recv.at[slot],
            device_id={"tensor": k}, device_id_type=MESH,
        )

    loop(size - 1, lambda j: send_scores((t + 1 + j) % size, t).start())

    def got(j):
        k = (t + 1 + j) % size
        send_scores(k, k).wait_recv()

    loop(size - 1, got)
    table = pieces[...].reshape(size * depth, 2 * examples)
    result = jnp.zeros(scores.shape, F32)
    hots = [
        jnp.where(
            lax.broadcasted_iota(jnp.int32, (size * depth, scores.shape[1]), 0) // depth * (2 * depth)
            + h * depth
            + lax.broadcasted_iota(jnp.int32, (size * depth, scores.shape[1]), 0) % depth
            == owner[...],
            1.0, 0.0,
        ).astype(BF16)
        for h in range(2)
    ]
    for _ in range(3):
        digit = table.astype(BF16)
        table = table - digit.astype(F32)
        for h in range(2):
            result = result + lax.dot_general(
                digit[:, h * examples:(h + 1) * examples], hots[h], (((0,), (0,)), ((), ())),
                preferred_element_type=F32,
            )
    scores[...] = result

    share_firsts(c).wait_send()
    loop(half, lambda k: across(k).wait_send())
    loop(half - 1, lambda j: along(peer(j), mine).wait_send())
    loop(half - 1, lambda j: to_peer(peer(j)).wait_send())
    loop(half - 2, lambda j: to_pair(peer(j)).wait_send())
    to_pair(mine).wait_send()
    if half > 1:
        to_diagonal().wait_send()
    loop(size, lambda k: to_core(k).wait_send())
    loop(size - 1, lambda j: send_scores((t + 1 + j) % size, t).wait_send())


def per_device(activations, out_grads, basis_in, basis_out, val_sketches, val_owner, example_ids):
    size = lax.axis_size("tensor")
    tokens, deep_in = activations.shape
    deep_out = out_grads.shape[1]
    rank = basis_in.shape[1]
    nblock = example_ids.shape[0]
    examples = nblock * lax.axis_size("context") // 2
    rows = tokens // size
    half = size // 2
    slots = max(8, rows // (tokens // nblock))
    stored, width = val_sketches.shape
    depth = max(8, stored // 2)
    if 2 * depth != stored:
        val_sketches = jnp.pad(val_sketches, ((0, 2 * depth - stored), (0, 0)))
        val_owner_at = val_owner // stored * (2 * depth) + val_owner % stored
    else:
        val_owner_at = val_owner
    vmem = pl.BlockSpec(memory_space=pltpu.VMEM)
    hbm = pl.BlockSpec(memory_space=pltpu.HBM)
    dma = pltpu.SemaphoreType.DMA
    return pl.pallas_call(
        functools.partial(kernel, size, slots),
        out_shape=(
            jax.ShapeDtypeStruct((examples, width), BF16),
            jax.ShapeDtypeStruct((examples, stored), F32),
        ),
        in_specs=[hbm] * 7,
        out_specs=(vmem, vmem),
        scratch_shapes=[
            pltpu.VMEM((BUFFERS, rows, deep_in), BF16),
            pltpu.VMEM((BUFFERS, rows, deep_out), BF16),
            pltpu.VMEM((2 * depth, width), BF16),
            pltpu.VMEM((1, stored), jnp.int32),
            pltpu.SMEM((nblock,), jnp.int32),
            pltpu.VMEM((2 * rank, deep_in), BF16),
            pltpu.VMEM((2 * rank, deep_out), BF16),
            pltpu.VMEM((size, rows, 2 * rank), BF16),
            pltpu.VMEM((half, rows, 2 * rank), BF16),
            pltpu.VMEM((half, rows, 2 * rank), BF16),
            pltpu.VMEM((rows, 2 * rank), F32),
            pltpu.VMEM((slots * rank // 2, 2 * rank), F32),
            pltpu.VMEM((2, 8, size * 2 * slots), jnp.int32),
            pltpu.VMEM((2 * size, 2 * slots, width // 2), BF16),
            pltpu.VMEM((size, depth, 2 * examples), F32),
            dma((BUFFERS,)), dma((BUFFERS,)), dma, dma, dma, dma, dma,
            dma((half,)), dma((half,)), dma((half,)), dma((half,)),
            dma, dma,
            dma((half,)), dma((half,)), dma((size,)), dma((2 * size,)),
            dma((size,)), dma((size,)),
        ],
        compiler_params=pltpu.CompilerParams(
            collective_id=0, has_side_effects=True, vmem_limit_bytes=48 * 1024 * 1024
        ),
        cost_estimate=pl.CostEstimate(
            flops=2 * tokens * (deep_in + deep_out) * rank,
            bytes_accessed=2 * tokens * (deep_in + deep_out),
            transcendentals=0,
        ),
    )(*[pltpu.with_memory_space_constraint(x, pltpu.HBM) for x in (activations, out_grads, basis_in.T, basis_out.T, val_sketches, val_owner_at.reshape(1, stored), example_ids)])


def solution(mesh):
    return jax.shard_map(
        per_device,
        mesh=mesh,
        in_specs=(
            P(("groups", "context"), "tensor"),
            P(("groups", "context"), "tensor"),
            P("tensor", None),
            P("tensor", None),
            P("tensor", None),
            P("tensor"),
            P(("groups", "context")),
        ),
        out_specs=(P("groups", None), P("groups", "tensor")),
        check_vma=False,
    )
```
